32 devices in a mesh: wide: 8 (over z, x), narrow: 4 (over y, core).
Axes of the slice: x: 2, y: 2, z: 4, core: 2. Of those that a mesh axis runs over, the one named last changes fastest.
Arguments:
- tensor: bfloat16 [32, 3, 1024, 1024], P('wide', None, 'narrow'), may hold values from -6 to 6
- occupied: bfloat16 [32, 3, 1024], replicated, may hold values from -0.625 to 0.625
- virtual: bfloat16 [32, 3, 1024], replicated, may hold values from -0.001953125 to 0.001953125
- atom_size: int32 [32], replicated, may hold values from 14 to 32, as said below
- tensor_pattern: int32 [32, 3], replicated, may hold values 0 or 1
- occupied_pattern: int32 [32, 3], replicated, may hold values 0 or 1
- virtual_pattern: int32 [32, 3], replicated, may hold values 0 or 1
Outputs:
- response: float32 [1024, 1024], P('wide', 'narrow')
The draws below stay inside these ranges and needn't reach their ends.
Inputs may be any that keep to these rules, and one draw needn't show every extreme that they name: Orbitals of an atom at and beyond its atom_size are padding.
All inputs are finite; a program needn't handle non-finite values.
Results may differ from the reference program's by a relative error of at most 0.0041.
Values may be sent and summed in bfloat16 or wider, within the bound.
A program may use at most 192 MiB of HBM per device.

```python
import jax
import jax.numpy as jnp
from jax import lax

BO = 32
NBAND = 3
PCH = 1024
NA = 32


def draw_atom_size(key, part):
    first_key, second_key = jax.random.split(key)
    lowest = BO * 7 // 16
    counts = jax.random.randint(first_key, (NA,), lowest, BO + 1, dtype=jnp.int32)
    order = jax.random.permutation(second_key, NA)
    counts = counts.at[order[0]].set(BO).at[order[1]].set(lowest)
    return counts


def with_ends(entries, own_key, smallest, high):
    longest = entries.shape.index(max(entries.shape))
    spots = []
    for shift in (0, 1):
        where = [jax.random.randint(jax.random.fold_in(own_key, axis), (), 0, length) for axis, length in enumerate(entries.shape)]
        where[longest] = (where[longest] + shift) % entries.shape[longest]
        spots.append(tuple(where))
    return entries.at[spots[0]].set(smallest).at[spots[1]].set(high)


def with_spikes(result, own_key, source, target, shards_of, factor):
    owner, partner = [(jnp.arange(result.shape[dim]) // (result.shape[dim] // shards_of)).reshape([-1 if axis == dim else 1 for axis in range(result.ndim)]) for dim in (source, target)]
    chosen = jax.random.permutation(own_key, shards_of)[partner]
    strong = (owner == chosen) | (owner == (partner + shards_of // 2) % shards_of)
    return jnp.where(strong, factor * result, result)


def block_levels(key, dims, cuts, low, top_value):
    def one(dim, parts):
        draws = jax.random.uniform(jax.random.fold_in(jax.random.fold_in(key, 6), dim), (parts,), jnp.float32, low / len(cuts), top_value / len(cuts))
        return jnp.repeat(jnp.exp(draws), dims[dim] // parts).reshape((-1,) + (1,) * (len(dims) - dim - 1))

    level = one(*cuts[0])
    for cut in cuts[1:]:
        level = level * one(*cut)
    return level


def normal_values(key, shape, deviation, reach, cuts=(), kind=jnp.bfloat16):
    drawn = deviation * jax.random.normal(key, shape, jnp.float32)
    if cuts:
        drawn = drawn * block_levels(key, shape, cuts, -0.22, 0.18)
    return jnp.clip(drawn, -reach, reach).astype(kind)


def noise_with(rng, dims, spread, limit, pieces, heavy, kind=jnp.bfloat16):
    result = spread * jax.random.normal(rng, dims, jnp.float32)
    if pieces:
        result = result * block_levels(rng, dims, pieces, -0.22, 0.18)
    return jnp.clip(with_spikes(result, jax.random.fold_in(rng, 3), *heavy), -limit, limit).astype(kind)


def setup_inputs(seed: int = 0) -> dict:
    key_of = jax.random.split(jax.random.key(seed), 8)
    return {
        "tensor": noise_with(key_of[0], (NA, NBAND, PCH, BO * BO), 1.0, 6.0, ((0, 8), (2, 4)), (0, 2, 8, 2.0)),
        "occupied": normal_values(key_of[1], (NA, NBAND, BO * BO), (NBAND * BO) ** -0.5, 0.625),
        "virtual": normal_values(key_of[2], (NA, NBAND, BO * BO), (NBAND * BO * NA * 5 * BO * BO // 2) ** -0.5, 0.001953125),
        "atom_size": draw_atom_size(jax.random.fold_in(key_of[7], 71), 0),
        "tensor_pattern": with_ends((jax.random.randint(key_of[4], (NA, NBAND), 0, 4) < 3).astype(jnp.int32), jax.random.fold_in(key_of[4], 1), 0, 1),
        "occupied_pattern": with_ends((jax.random.randint(key_of[5], (NA, NBAND), 0, 4) < 3).astype(jnp.int32), jax.random.fold_in(key_of[5], 1), 0, 1),
        "virtual_pattern": with_ends((jax.random.randint(key_of[6], (NA, NBAND), 0, 4) < 3).astype(jnp.int32), jax.random.fold_in(key_of[6], 1), 0, 1),
    }


def block_masks(size_pad, tensor_flags, occupied_flags, virtual_flags, atom_index):
    nearby_sizes = lax.dynamic_slice(size_pad, (atom_index,), (5,))
    present = (nearby_sizes > 0).astype(jnp.int32)
    orbital = jnp.arange(BO, dtype=jnp.int32)
    zero_index = jnp.zeros((), jnp.int32)
    row_flags = lax.dynamic_slice(tensor_flags, (atom_index + 1, zero_index), (3, 3))
    row_ok = (orbital[None, :] < nearby_sizes[1:4, None]).astype(jnp.int32)
    partner = jnp.stack([nearby_sizes[r:r + 3] for r in range(3)])
    column_ok = (orbital[None, None, :] < partner[:, :, None]).astype(jnp.int32)
    entry_mask = row_flags[:, :, None, None] * row_ok[:, None, :, None] * column_ok[:, :, None, :]
    tensor_mask = entry_mask.reshape(3, 3, 1, BO * BO).astype(jnp.bfloat16)
    occupied_mask = lax.dynamic_slice(occupied_flags, (atom_index + 2, zero_index), (1, 3))[0] * present[1:4]
    partner_present = jnp.stack([present[r:r + 3] for r in range(3)])
    virtual_mask = lax.dynamic_slice(virtual_flags, (atom_index + 1, zero_index), (3, 3)) * present[1:4, None] * partner_present
    return tensor_mask, occupied_mask.astype(jnp.bfloat16), virtual_mask.astype(jnp.bfloat16)


def contract(row_blocks, occupied_row, virtual_rows):
    ri_count = row_blocks.shape[2]
    blocks = row_blocks.reshape(3, 3, ri_count, BO, BO).astype(jnp.float32)
    occupied_blocks = occupied_row.reshape(3, BO, BO).astype(jnp.float32)
    virtual_blocks = virtual_rows.reshape(3, 3, BO, BO).astype(jnp.float32)
    occupied_terms = []
    virtual_terms = []
    for out_band in range(5):
        total_left = jnp.zeros((ri_count, BO, BO), jnp.float32)
        total_right = jnp.zeros((ri_count, BO, BO), jnp.float32)
        for left_band in range(3):
            right_band = out_band - left_band
            if 0 <= right_band < 3:
                total_left = total_left + jnp.einsum('lm,pmn->pln', occupied_blocks[left_band], blocks[left_band, right_band])
                total_right = total_right + jnp.einsum('pls,sn->pln', blocks[1, left_band], virtual_blocks[left_band, right_band])
        occupied_terms.append(total_left.reshape(ri_count, BO * BO))
        virtual_terms.append(total_right.reshape(ri_count, BO * BO))
    left_product = jnp.stack(occupied_terms, 1).reshape(ri_count, 5 * BO * BO).astype(jnp.bfloat16)
    right_product = jnp.stack(virtual_terms, 1).reshape(ri_count, 5 * BO * BO).astype(jnp.bfloat16)
    return left_product, right_product


def reference(tensor, occupied, virtual, atom_size, tensor_pattern, occupied_pattern, virtual_pattern):
    padded = jnp.pad(tensor, ((1, 1), (0, 0), (0, 0), (0, 0)))
    occupied_pad = jnp.pad(occupied, ((1, 1), (0, 0), (0, 0)))
    virtual_pad = jnp.pad(virtual, ((1, 1), (0, 0), (0, 0)))
    size_pad = jnp.pad(atom_size, 2)
    tensor_flags = jnp.pad(tensor_pattern, ((2, 2), (0, 0)))
    occupied_flags = jnp.pad(occupied_pattern, ((2, 2), (0, 0)))
    virtual_flags = jnp.pad(virtual_pattern, ((2, 2), (0, 0)))

    def advance(response, atom_index):
        row_blocks = lax.dynamic_slice_in_dim(padded, atom_index, 3, 0)
        tensor_mask, occupied_mask, virtual_mask = block_masks(size_pad, tensor_flags, occupied_flags, virtual_flags, atom_index)
        row_blocks = row_blocks * tensor_mask
        occupied_row = lax.dynamic_slice_in_dim(occupied_pad, atom_index + 1, 1, 0)[0] * occupied_mask[:, None]
        virtual_rows = lax.dynamic_slice_in_dim(virtual_pad, atom_index, 3, 0) * virtual_mask[:, :, None]
        left_product, right_product = contract(row_blocks, occupied_row, virtual_rows)
        return response + jnp.dot(left_product, right_product.T, preferred_element_type=jnp.float32), None

    response, unused = lax.scan(advance, jnp.zeros((PCH, PCH), jnp.float32), jnp.arange(NA, dtype=jnp.int32))
    return response
```

```python
import jax
import jax.numpy as jnp
from jax import lax
from jax.experimental import pallas as pl
from jax.experimental.pallas import tpu as pltpu
from jax.sharding import PartitionSpec as P

BO = 32
LANES = BO * BO
GROUP = 256
VMEM_LIMIT = 56 * 1024 * 1024


def weight_kernel(before, here, after, mask, kron_v, occ_cols, delta, out, kron_o, right, total):
    i = pl.program_id(0)
    ri = here.shape[2]
    for co, rows in enumerate((before, here, after)):
        for lam in range(BO):
            kron_o[lam * BO : (lam + 1) * BO, :] = occ_cols[0, co, lam : lam + 1, :] * delta[...]
        blocks = [rows[0, ds] * mask[i + co, ds : ds + 1, :] for ds in range(3)]
        for bo in range(3):
            for g in range(LANES // GROUP):
                lanes = slice(g * GROUP, (g + 1) * GROUP)
                acc = None
                for ds in range(3):
                    e = bo + 2 - (co + ds)
                    if 0 <= e < 3:
                        term = jnp.dot(
                            blocks[ds][:, lanes],
                            kron_v[i + co + ds, e],
                            preferred_element_type=jnp.float32,
                        )
                        acc = term if acc is None else acc + term
                right[bo * ri : (bo + 1) * ri, lanes] = acc.astype(jnp.bfloat16)
        product = jnp.dot(right[...], kron_o[...], preferred_element_type=jnp.float32)
        if co == 0:
            total[...] = product
        elif co == 1:
            total[...] += product
        else:
            for bo in range(3):
                rows_of = slice(bo * ri, (bo + 1) * ri)
                value = total[rows_of, :] + product[rows_of, :]
                keep = mask[i + 1, bo : bo + 1, :].astype(jnp.float32)
                out[0, bo] = (value * keep).astype(jnp.bfloat16)


def weights(rows, mask, kron_v, occ_cols, delta):
    atoms = rows.shape[0] - 2
    ri = rows.shape[2]
    row_spec = lambda shift: pl.BlockSpec((1, 3, ri, LANES), lambda i, s=shift: (i + s, 0, 0, 0))
    full = lambda a: pl.BlockSpec(a.shape, lambda i, r=a.ndim: (0,) * r)
    flops = atoms * 2 * ri * LANES * (19 * GROUP + 9 * LANES)
    return pl.pallas_call(
        weight_kernel,
        grid=(atoms,),
        out_shape=jax.ShapeDtypeStruct((atoms, 3, ri, LANES), jnp.bfloat16),
        in_specs=[
            row_spec(0),
            row_spec(1),
            row_spec(2),
            full(mask),
            full(kron_v),
            pl.BlockSpec((1, 3, BO, LANES), lambda i: (i, 0, 0, 0)),
            full(delta),
        ],
        out_specs=pl.BlockSpec((1, 3, ri, LANES), lambda i: (i, 0, 0, 0)),
        scratch_shapes=[
            pltpu.VMEM((LANES, LANES), jnp.bfloat16),
            pltpu.VMEM((3 * ri, LANES), jnp.bfloat16),
            pltpu.VMEM((3 * ri, LANES), jnp.float32),
        ],
        compiler_params=pltpu.CompilerParams(vmem_limit_bytes=VMEM_LIMIT),
        cost_estimate=pl.CostEstimate(
            flops=flops, bytes_accessed=4 * rows.size * 2, transcendentals=0
        ),
    )(rows, rows, rows, mask, kron_v, occ_cols, delta)


def response_kernel(first, second, weight, out):
    ri = first.shape[2]

    @pl.when(pl.program_id(0) == 0)
    def _():
        out[...] = jnp.zeros_like(out)

    for half, left in enumerate((first, second)):
        total = None
        for b in range(3):
            term = lax.dot_general(
                left[0, b],
                weight[0, b],
                (((1,), (1,)), ((), ())),
                preferred_element_type=jnp.float32,
            )
            total = term if total is None else total + term
        out[half] += total


def responses(first, second, weight, start):
    atoms, _, ri, _ = first.shape
    spec = lambda shift: pl.BlockSpec((1, 3, ri, LANES), lambda i, s=shift: (i + s, 0, 0, 0))
    return pl.pallas_call(
        response_kernel,
        grid=(atoms,),
        out_shape=jax.ShapeDtypeStruct((2, ri, ri), jnp.float32),
        in_specs=[spec(0), spec(0), spec(start)],
        out_specs=pl.BlockSpec((2, ri, ri), lambda i: (0, 0, 0)),
        compiler_params=pltpu.CompilerParams(vmem_limit_bytes=VMEM_LIMIT),
        cost_estimate=pl.CostEstimate(
            flops=atoms * 12 * ri * ri * LANES,
            bytes_accessed=atoms * 9 * ri * LANES * 2,
            transcendentals=0,
        ),
    )(first, second, weight)


def small_tables(occupied, virtual, atom_size, tensor_pattern, occupied_pattern, virtual_pattern, atoms):
    first = lax.axis_index("wide") * atoms
    total = atom_size.shape[0]

    def near(array, margin):
        pads = ((margin, margin),) + ((0, 0),) * (array.ndim - 1)
        return lax.dynamic_slice_in_dim(jnp.pad(array, pads), first, atoms + 2 * margin, 0)

    def partners(margin):
        own = first - margin + jnp.arange(atoms + 2 * margin)
        other = own[:, None] + jnp.arange(-1, 2)[None, :]
        return ((own >= 0) & (own < total))[:, None] & (other >= 0) & (other < total)

    sizes = near(atom_size, 2)
    count = atoms + 2
    flags = (near(tensor_pattern, 1) != 0) & partners(1)
    partner = jnp.stack([sizes[d : d + count] for d in range(3)], 1)
    lane = jnp.arange(LANES, dtype=jnp.int32)
    row_ok = (lane // BO)[None, None, :] < sizes[1 : 1 + count, None, None]
    column_ok = (lane % BO)[None, None, :] < partner[:, :, None]
    mask = (flags[:, :, None] & row_ok & column_ok).astype(jnp.bfloat16)

    occ_keep = ((near(occupied_pattern, 1) != 0) & partners(1)).astype(jnp.bfloat16)
    occ = near(occupied, 1) * occ_keep[:, :, None]
    occ = jnp.stack([occ[co : co + atoms, 2 - co] for co in range(3)], 1)
    occ = occ.reshape(atoms, 3, BO, BO)
    spread = (lane[None, :] // BO == jnp.arange(BO)[:, None]).astype(jnp.bfloat16)
    occ_cols = jnp.einsum(
        "acij,jl->acil", occ, spread, preferred_element_type=jnp.float32
    ).astype(jnp.bfloat16)
    delta = (lane[None, :] % BO == jnp.arange(BO)[:, None]).astype(jnp.bfloat16)

    vir_keep = ((near(virtual_pattern, 2) != 0) & partners(2)).astype(jnp.bfloat16)
    vir = (near(virtual, 2) * vir_keep[:, :, None]).reshape(atoms + 4, 3, BO, BO)
    short = jnp.arange(GROUP)
    same = (short[:, None] // BO == short[None, :] // BO).astype(jnp.bfloat16)
    kron_v = jnp.tile(vir, (1, 1, GROUP // BO, GROUP // BO)) * same
    return mask, occ_cols, delta, kron_v


def body(tensor, occupied, virtual, atom_size, tensor_pattern, occupied_pattern, virtual_pattern):
    wide = lax.axis_size("wide")
    narrow = lax.axis_size("narrow")
    atoms, _, ri, _ = tensor.shape
    me = lax.axis_index("narrow")
    up = [(i, i + 1) for i in range(wide - 1)]
    down = [(i + 1, i) for i in range(wide - 1)]
    sibling = [(i, i ^ 1) for i in range(narrow)]
    before = lax.ppermute(tensor[atoms - 1 :], "wide", up)
    after = lax.ppermute(tensor[:1], "wide", down)
    near = lax.ppermute(tensor, "narrow", sibling)
    far = []
    for step in range(2, narrow, 2):
        pairs = [(i, (i + step) % narrow) for i in range(narrow)]
        for a in range(atoms):
            direct = lax.ppermute(tensor[a : a + 1], "narrow", pairs)
            passed = lax.ppermute(direct, "narrow", sibling)
            far.append((step, a, direct, passed))

    mask, occ_cols, delta, kron_v = small_tables(
        occupied, virtual, atom_size, tensor_pattern, occupied_pattern, virtual_pattern, atoms
    )
    rows = jnp.concatenate([before, tensor, after], 0)
    weight = weights(rows, mask, kron_v, occ_cols, delta)
    parts = {0: responses(tensor, near, weight, 0)}
    for step, a, direct, passed in far:
        part = responses(direct, passed, weight, a)
        parts[step] = parts[step] + part if step in parts else part

    core = me % 2
    ordered = []
    for pair in range(narrow // 2):
        step = (me // 2 - pair) % (narrow // 2) * 2
        block = parts[0]
        for s in range(2, narrow, 2):
            block = jnp.where(step == s, parts[s], block)
        ordered.append(jnp.where(core == 0, block, block[::-1]))
    partial = jnp.concatenate(ordered, 0).reshape(wide, narrow * ri // wide, ri)
    shares = lax.all_to_all(partial.astype(jnp.bfloat16), "wide", 0, 0, tiled=True)
    return jnp.sum(shares.astype(jnp.float32), 0)


def solution(mesh):
    placed = (P("wide", None, "narrow", None), P(), P(), P(), P(), P(), P())
    return jax.shard_map(
        body, mesh=mesh, in_specs=placed, out_specs=P("wide", "narrow"), check_vma=False
    )
```

```python
import functools

import jax
import jax.numpy as jnp
from jax import lax
from jax.experimental import pallas as pl
from jax.experimental.pallas import tpu as pltpu
from jax.sharding import PartitionSpec as P

BO = 32
LANES = BO * BO
GROUP = 256
TILE = 128
FRACTIONS = (8, 9, 10, 11, 12)
VMEM_LIMIT = 56 * 1024 * 1024
SMALL = pl.CostEstimate(flops=1, bytes_accessed=1, transcendentals=0)


def weight_kernel(base, before, here, after, mask, kron_v, occ_cols, delta, *rest):
    out, kron_o, right, total = rest[-4:]
    i = pl.program_id(0) + base
    ri = here.shape[2]
    for co, rows in enumerate((before, here, after)):
        for lam in range(BO):
            kron_o[lam * BO : (lam + 1) * BO, :] = occ_cols[0, co, lam : lam + 1, :] * delta[...]
        blocks = [rows[0, ds] * mask[i + co, ds : ds + 1, :] for ds in range(3)]
        for bo in range(3):
            for g in range(LANES // GROUP):
                lanes = slice(g * GROUP, (g + 1) * GROUP)
                acc = None
                for ds in range(3):
                    e = bo + 2 - (co + ds)
                    if 0 <= e < 3:
                        term = jnp.dot(
                            blocks[ds][:, lanes],
                            kron_v[i + co + ds, e],
                            preferred_element_type=jnp.float32,
                        )
                        acc = term if acc is None else acc + term
                right[bo * ri : (bo + 1) * ri, lanes] = acc.astype(jnp.bfloat16)
        product = jnp.dot(right[...], kron_o[...], preferred_element_type=jnp.float32)
        if co == 0:
            total[...] = product
        elif co == 1:
            total[...] += product
        else:
            for bo in range(3):
                rows_of = slice(bo * ri, (bo + 1) * ri)
                value = total[rows_of, :] + product[rows_of, :]
                keep = mask[i + 1, bo : bo + 1, :].astype(jnp.float32)
                out[0, bo] = (value * keep).astype(jnp.bfloat16)


def weights(arrays, starts, base, count, atoms, mask, kron_v, occ_cols, delta, held=None):
    ri = arrays[0].shape[2]
    row_spec = lambda shift: pl.BlockSpec((1, 3, ri, LANES), lambda i, s=shift: (i + s, 0, 0, 0))
    full = lambda a: pl.BlockSpec(a.shape, lambda i, r=a.ndim: (0,) * r)
    operands = [*arrays, mask, kron_v, occ_cols, delta]
    specs = [row_spec(start) for start in starts] + [
        full(mask),
        full(kron_v),
        pl.BlockSpec((1, 3, BO, LANES), lambda i: (i + base, 0, 0, 0)),
        full(delta),
    ]
    aliases = {}
    if held is not None:
        aliases = {len(operands): 0}
        operands.append(held)
        specs.append(pl.BlockSpec(memory_space=pl.ANY))
    return pl.pallas_call(
        functools.partial(weight_kernel, base),
        grid=(count,),
        out_shape=jax.ShapeDtypeStruct((atoms, 3, ri, LANES), jnp.bfloat16),
        in_specs=specs,
        out_specs=pl.BlockSpec((1, 3, ri, LANES), lambda i: (i + base, 0, 0, 0)),
        scratch_shapes=[
            pltpu.VMEM((LANES, LANES), jnp.bfloat16),
            pltpu.VMEM((3 * ri, LANES), jnp.bfloat16),
            pltpu.VMEM((3 * ri, LANES), jnp.float32),
        ],
        input_output_aliases=aliases,
        compiler_params=pltpu.CompilerParams(vmem_limit_bytes=VMEM_LIMIT),
        cost_estimate=SMALL,
    )(*operands)


def pack_kernel(order, source, out, sem):
    @pl.loop(0, out.shape[0])
    def _(j):
        index = order[j]
        lanes = pl.ds(pl.multiple_of((index % 8) * TILE, TILE), TILE)
        pltpu.make_async_copy(source.at[index // 8, :, lanes], out.at[j], sem).start()

    pltpu.make_async_copy(out, out, sem).wait()


def pack(order, source):
    ri = source.shape[1]
    return pl.pallas_call(
        pack_kernel,
        out_shape=jax.ShapeDtypeStruct((order.shape[0], ri, TILE), jnp.bfloat16),
        in_specs=[pl.BlockSpec(memory_space=pltpu.SMEM), pl.BlockSpec(memory_space=pl.ANY)],
        out_specs=pl.BlockSpec(memory_space=pl.ANY),
        scratch_shapes=[pltpu.SemaphoreType.DMA],
        compiler_params=pltpu.CompilerParams(vmem_limit_bytes=VMEM_LIMIT),
        cost_estimate=SMALL,
    )(order, source)


def packed_kernel(order, left, weight, out):
    step = pl.program_id(0)

    @pl.when(step == 0)
    def _():
        out[...] = jnp.zeros_like(out)

    def tile(u):
        index = order[step * 8 + u]
        lanes = pl.ds(pl.multiple_of((index % 8) * TILE, TILE), TILE)
        return weight[index // 8, :, lanes]

    total = None
    for u in range(0, 8, 2):
        term = lax.dot_general(
            jnp.concatenate([left[u], left[u + 1]], 1),
            jnp.concatenate([tile(u), tile(u + 1)], 1),
            (((1,), (1,)), ((), ())),
            preferred_element_type=jnp.float32,
        )
        total = term if total is None else total + term
    out[...] += total


def packed_responses(order, left, weight):
    tiles, ri, _ = left.shape
    spec = pl.BlockSpec((8, ri, TILE), lambda i: (i, 0, 0))
    return pl.pallas_call(
        packed_kernel,
        grid=(tiles // 8,),
        out_shape=jax.ShapeDtypeStruct((ri, ri), jnp.float32),
        in_specs=[
            pl.BlockSpec(memory_space=pltpu.SMEM),
            spec,
            pl.BlockSpec(weight.shape, lambda i: (0, 0, 0)),
        ],
        out_specs=pl.BlockSpec((ri, ri), lambda i: (0, 0)),
        compiler_params=pltpu.CompilerParams(vmem_limit_bytes=VMEM_LIMIT),
        cost_estimate=SMALL,
    )(order, left, weight)


def response_kernel(first, second, weight, out):
    ri = first.shape[2]

    @pl.when(pl.program_id(0) == 0)
    def _():
        out[...] = jnp.zeros_like(out)

    for half, left in enumerate((first, second)):
        total = None
        for b in range(3):
            term = lax.dot_general(
                left[0, b],
                weight[0, b],
                (((1,), (1,)), ((), ())),
                preferred_element_type=jnp.float32,
            )
            total = term if total is None else total + term
        out[half] += total


def responses(first, second, weight):
    atoms, _, ri, _ = first.shape
    spec = pl.BlockSpec((1, 3, ri, LANES), lambda i: (i, 0, 0, 0))
    return pl.pallas_call(
        response_kernel,
        grid=(atoms,),
        out_shape=jax.ShapeDtypeStruct((2, ri, ri), jnp.float32),
        in_specs=[spec, spec, spec],
        out_specs=pl.BlockSpec((2, ri, ri), lambda i: (0, 0, 0)),
        compiler_params=pltpu.CompilerParams(vmem_limit_bytes=VMEM_LIMIT),
        cost_estimate=SMALL,
    )(first, second, weight)


def small_tables(occupied, virtual, atom_size, tensor_pattern, occupied_pattern, virtual_pattern, atoms):
    first = lax.axis_index("wide") * atoms
    total = atom_size.shape[0]

    def near(array, margin):
        pads = ((margin, margin),) + ((0, 0),) * (array.ndim - 1)
        return lax.dynamic_slice_in_dim(jnp.pad(array, pads), first, atoms + 2 * margin, 0)

    def partners(margin):
        own = first - margin + jnp.arange(atoms + 2 * margin)
        other = own[:, None] + jnp.arange(-1, 2)[None, :]
        return ((own >= 0) & (own < total))[:, None] & (other >= 0) & (other < total)

    sizes = near(atom_size, 2)
    count = atoms + 2
    flags = (near(tensor_pattern, 1) != 0) & partners(1)
    partner = jnp.stack([sizes[d : d + count] for d in range(3)], 1)
    lane = jnp.arange(LANES, dtype=jnp.int32)
    row_ok = (lane // BO)[None, None, :] < sizes[1 : 1 + count, None, None]
    column_ok = (lane % BO)[None, None, :] < partner[:, :, None]
    mask = (flags[:, :, None] & row_ok & column_ok).astype(jnp.bfloat16)

    occ_keep = ((near(occupied_pattern, 1) != 0) & partners(1)).astype(jnp.bfloat16)
    occ = near(occupied, 1) * occ_keep[:, :, None]
    occ = jnp.stack([occ[co : co + atoms, 2 - co] for co in range(3)], 1)
    occ = occ.reshape(atoms, 3, BO, BO)
    spread = (lane[None, :] // BO == jnp.arange(BO)[:, None]).astype(jnp.bfloat16)
    occ_cols = jnp.einsum(
        "acij,jl->acil", occ, spread, preferred_element_type=jnp.float32
    ).astype(jnp.bfloat16)
    delta = (lane[None, :] % BO == jnp.arange(BO)[:, None]).astype(jnp.bfloat16)

    vir_keep = ((near(virtual_pattern, 2) != 0) & partners(2)).astype(jnp.bfloat16)
    vir = (near(virtual, 2) * vir_keep[:, :, None]).reshape(atoms + 4, 3, BO, BO)
    short = jnp.arange(GROUP, dtype=jnp.int32)
    spread = (short[None, :] % BO == jnp.arange(BO)[:, None]).astype(jnp.bfloat16)
    cols = jnp.einsum(
        "seij,jl->seil", vir, spread, preferred_element_type=jnp.float32
    ).astype(jnp.bfloat16)
    same = (short[None, :] // BO == jnp.arange(GROUP // BO)[:, None]).astype(jnp.bfloat16)
    kron_v = (cols[:, :, None] * same[None, None, :, None, :]).reshape(atoms + 4, 3, GROUP, GROUP)
    return mask, kron_v, occ_cols, delta


def tile_lists(atom_size, tensor_pattern, atoms):
    total = atom_size.shape[0]
    other = jnp.arange(total)[:, None] + jnp.arange(-1, 2)[None, :]
    flags = (tensor_pattern != 0) & (other >= 0) & (other < total)
    low = jnp.arange(LANES // TILE, dtype=jnp.int32) * (TILE // BO)
    used = flags[:, :, None] & (low[None, None, :] < atom_size[:, None, None])
    used = used.reshape(total // atoms, atoms * 3 * LANES // TILE).astype(jnp.int32)
    largest = jnp.max(jnp.sum(used, 1))
    mine = lax.dynamic_index_in_dim(used, lax.axis_index("wide"), 0, keepdims=False)
    place = jnp.where(
        mine == 1, jnp.cumsum(mine) - 1, jnp.sum(mine) + jnp.cumsum(1 - mine) - 1
    )
    spots = jnp.arange(mine.shape[0], dtype=jnp.int32)
    order = jnp.sum(jnp.where(place[None, :] == spots[:, None], spots[None, :], 0), 1)
    return order.astype(jnp.int32), largest


def partial_response(tiles, tensor, order, *small):
    wide = lax.axis_size("wide")
    narrow = lax.axis_size("narrow")
    atoms, _, ri, _ = tensor.shape
    me = lax.axis_index("narrow")
    up = [(i, i + 1) for i in range(wide - 1)]
    down = [(i + 1, i) for i in range(wide - 1)]
    sibling = [(i, i ^ 1) for i in range(narrow)]
    after_of = lax.optimization_barrier
    order = order[:tiles]
    packed = pack(order, tensor.reshape(atoms * 3, ri, LANES))
    packed, tensor = after_of((packed, tensor))
    direct = {}
    for step in range(2, narrow, 2):
        pairs = [(i, (i + step) % narrow) for i in range(narrow)]
        direct[step] = lax.ppermute(packed, "narrow", pairs)
    before = lax.ppermute(tensor[atoms - 1 :], "wide", up)
    after = lax.ppermute(tensor[:1], "wide", down)
    near = lax.ppermute(tensor, "narrow", sibling)

    tables = small_tables(*small, atoms)
    weight = weights((tensor,) * 3, (0, 1, 2), 1, atoms - 2, atoms, *tables)
    before, after, weight = after_of((before, after, weight))
    weight = weights((before, tensor, tensor), (0, 0, 1), 0, 1, atoms, *tables, weight)
    weight = weights(
        (tensor, tensor, after), (atoms - 2, atoms - 1, 0), atoms - 1, 1, atoms, *tables, weight
    )
    near, weight = after_of((near, weight))
    flat = weight.reshape(atoms * 3, ri, LANES)
    own = responses(tensor, near, weight)
    parts = {0: own}
    for step, held in direct.items():
        held, own, flat = after_of((held, own, flat))
        passed = lax.ppermute(held, "narrow", sibling)
        first = packed_responses(order, held, flat)
        passed, first, flat = after_of((passed, first, flat))
        second = packed_responses(order, passed, flat)
        own = second
        parts[step] = jnp.stack([first, second])

    core = me % 2
    ordered = []
    for pair in range(narrow // 2):
        step = (me // 2 - pair) % (narrow // 2) * 2
        block = parts[0]
        for s in range(2, narrow, 2):
            block = jnp.where(step == s, parts[s], block)
        ordered.append(jnp.where(core == 0, block, block[::-1]))
    partial = jnp.concatenate(ordered, 0).reshape(wide, narrow * ri // wide, ri)
    return partial.astype(jnp.bfloat16)


def body(tensor, occupied, virtual, atom_size, tensor_pattern, occupied_pattern, virtual_pattern):
    atoms = tensor.shape[0]
    order, largest = tile_lists(atom_size, tensor_pattern, atoms)
    every = order.shape[0]
    counts = [every * f // 12 // 8 * 8 for f in FRACTIONS]
    branch = sum((largest > n).astype(jnp.int32) for n in counts[:-1])
    partial = lax.switch(
        branch,
        [functools.partial(partial_response, n) for n in counts],
        tensor,
        order,
        occupied,
        virtual,
        atom_size,
        tensor_pattern,
        occupied_pattern,
        virtual_pattern,
    )
    shares = lax.all_to_all(partial, "wide", 0, 0, tiled=True)
    return jnp.sum(shares.astype(jnp.float32), 0)


def solution(mesh):
    placed = (P("wide", None, "narrow", None), P(), P(), P(), P(), P(), P())
    return jax.shard_map(
        body, mesh=mesh, in_specs=placed, out_specs=P("wide", "narrow"), check_vma=False
    )
```

```python
import functools

import jax
import jax.numpy as jnp
from jax import lax
from jax.experimental import pallas as pl
from jax.experimental.pallas import tpu as pltpu
from jax.sharding import PartitionSpec as P

BO = 32
LANES = BO * BO
GROUP = 256
VMEM_LIMIT = 56 * 1024 * 1024
SMALL = pl.CostEstimate(flops=1, bytes_accessed=1, transcendentals=0)


def weight_kernel(base, before, here, after, mask, kron_v, occ_cols, delta, *rest):
    out, kron_o, right, total = rest[-4:]
    i = pl.program_id(0) + base
    ri = here.shape[2]
    for co, rows in enumerate((before, here, after)):
        for lam in range(BO):
            kron_o[lam * BO : (lam + 1) * BO, :] = occ_cols[0, co, lam : lam + 1, :] * delta[...]
        blocks = [rows[0, ds] * mask[i + co, ds : ds + 1, :] for ds in range(3)]
        for bo in range(3):
            for g in range(LANES // GROUP):
                lanes = slice(g * GROUP, (g + 1) * GROUP)
                acc = None
                for ds in range(3):
                    e = bo + 2 - (co + ds)
                    if 0 <= e < 3:
                        term = jnp.dot(
                            blocks[ds][:, lanes],
                            kron_v[i + co + ds, e],
                            preferred_element_type=jnp.float32,
                        )
                        acc = term if acc is None else acc + term
                right[bo * ri : (bo + 1) * ri, lanes] = acc.astype(jnp.bfloat16)
        product = jnp.dot(right[...], kron_o[...], preferred_element_type=jnp.float32)
        if co == 0:
            total[...] = product
        elif co == 1:
            total[...] += product
        else:
            for bo in range(3):
                rows_of = slice(bo * ri, (bo + 1) * ri)
                value = total[rows_of, :] + product[rows_of, :]
                keep = mask[i + 1, bo : bo + 1, :].astype(jnp.float32)
                out[0, bo] = (value * keep).astype(jnp.bfloat16)


def weights(arrays, starts, base, count, atoms, mask, kron_v, occ_cols, delta, held=None):
    ri = arrays[0].shape[2]
    row_spec = lambda shift: pl.BlockSpec((1, 3, ri, LANES), lambda i, s=shift: (i + s, 0, 0, 0))
    full = lambda a: pl.BlockSpec(a.shape, lambda i, r=a.ndim: (0,) * r)
    operands = [*arrays, mask, kron_v, occ_cols, delta]
    specs = [row_spec(start) for start in starts] + [
        full(mask),
        full(kron_v),
        pl.BlockSpec((1, 3, BO, LANES), lambda i: (i + base, 0, 0, 0)),
        full(delta),
    ]
    aliases = {}
    if held is not None:
        aliases = {len(operands): 0}
        operands.append(held)
        specs.append(pl.BlockSpec(memory_space=pl.ANY))
    return pl.pallas_call(
        functools.partial(weight_kernel, base),
        grid=(count,),
        out_shape=jax.ShapeDtypeStruct((atoms, 3, ri, LANES), jnp.bfloat16),
        in_specs=specs,
        out_specs=pl.BlockSpec((1, 3, ri, LANES), lambda i: (i + base, 0, 0, 0)),
        scratch_shapes=[
            pltpu.VMEM((LANES, LANES), jnp.bfloat16),
            pltpu.VMEM((3 * ri, LANES), jnp.bfloat16),
            pltpu.VMEM((3 * ri, LANES), jnp.float32),
        ],
        input_output_aliases=aliases,
        compiler_params=pltpu.CompilerParams(vmem_limit_bytes=VMEM_LIMIT),
        cost_estimate=SMALL,
    )(*operands)


def response_kernel(left, weight, out):
    @pl.when(pl.program_id(0) == 0)
    def _():
        out[...] = jnp.zeros_like(out)

    total = None
    for b in range(3):
        term = lax.dot_general(
            left[0, b],
            weight[0, b],
            (((1,), (1,)), ((), ())),
            preferred_element_type=jnp.float32,
        )
        total = term if total is None else total + term
    out[...] += total


def responses(left, weight):
    atoms, _, ri, _ = left.shape
    spec = pl.BlockSpec((1, 3, ri, LANES), lambda i: (i, 0, 0, 0))
    return pl.pallas_call(
        response_kernel,
        grid=(atoms,),
        out_shape=jax.ShapeDtypeStruct((ri, ri), jnp.float32),
        in_specs=[spec, spec],
        out_specs=pl.BlockSpec((ri, ri), lambda i: (0, 0)),
        compiler_params=pltpu.CompilerParams(vmem_limit_bytes=VMEM_LIMIT),
        cost_estimate=SMALL,
    )(left, weight)


def small_tables(occupied, virtual, atom_size, tensor_pattern, occupied_pattern, virtual_pattern, atoms):
    first = lax.axis_index("wide") * atoms
    total = atom_size.shape[0]

    def near(array, margin):
        pads = ((margin, margin),) + ((0, 0),) * (array.ndim - 1)
        return lax.dynamic_slice_in_dim(jnp.pad(array, pads), first, atoms + 2 * margin, 0)

    def partners(margin):
        own = first - margin + jnp.arange(atoms + 2 * margin)
        other = own[:, None] + jnp.arange(-1, 2)[None, :]
        return ((own >= 0) & (own < total))[:, None] & (other >= 0) & (other < total)

    sizes = near(atom_size, 2)
    count = atoms + 2
    flags = (near(tensor_pattern, 1) != 0) & partners(1)
    partner = jnp.stack([sizes[d : d + count] for d in range(3)], 1)
    lane = jnp.arange(LANES, dtype=jnp.int32)
    row_ok = (lane // BO)[None, None, :] < sizes[1 : 1 + count, None, None]
    column_ok = (lane % BO)[None, None, :] < partner[:, :, None]
    mask = (flags[:, :, None] & row_ok & column_ok).astype(jnp.bfloat16)

    occ_keep = ((near(occupied_pattern, 1) != 0) & partners(1)).astype(jnp.bfloat16)
    occ = near(occupied, 1) * occ_keep[:, :, None]
    occ = jnp.stack([occ[co : co + atoms, 2 - co] for co in range(3)], 1)
    occ = occ.reshape(atoms, 3, BO, BO)
    spread = (lane[None, :] // BO == jnp.arange(BO)[:, None]).astype(jnp.bfloat16)
    occ_cols = jnp.einsum(
        "acij,jl->acil", occ, spread, preferred_element_type=jnp.float32
    ).astype(jnp.bfloat16)
    delta = (lane[None, :] % BO == jnp.arange(BO)[:, None]).astype(jnp.bfloat16)

    vir_keep = ((near(virtual_pattern, 2) != 0) & partners(2)).astype(jnp.bfloat16)
    vir = (near(virtual, 2) * vir_keep[:, :, None]).reshape(atoms + 4, 3, BO, BO)
    short = jnp.arange(GROUP, dtype=jnp.int32)
    spread = (short[None, :] % BO == jnp.arange(BO)[:, None]).astype(jnp.bfloat16)
    cols = jnp.einsum(
        "seij,jl->seil", vir, spread, preferred_element_type=jnp.float32
    ).astype(jnp.bfloat16)
    same = (short[None, :] // BO == jnp.arange(GROUP // BO)[:, None]).astype(jnp.bfloat16)
    kron_v = (cols[:, :, None] * same[None, None, :, None, :]).reshape(atoms + 4, 3, GROUP, GROUP)
    return mask, kron_v, occ_cols, delta


def partial_response(tensor, *small):
    wide = lax.axis_size("wide")
    narrow = lax.axis_size("narrow")
    atoms, _, ri, _ = tensor.shape
    me = lax.axis_index("narrow")
    up = [(i, i + 1) for i in range(wide - 1)]
    down = [(i + 1, i) for i in range(wide - 1)]
    sibling = [(i, i ^ 1) for i in range(narrow)]
    after_of = lax.optimization_barrier
    direct = {}
    for step in range(2, narrow, 2):
        pairs = [(i, (i + step) % narrow) for i in range(narrow)]
        direct[step] = lax.ppermute(tensor, "narrow", pairs)
    before = lax.ppermute(tensor[atoms - 1 :], "wide", up)
    after = lax.ppermute(tensor[:1], "wide", down)
    near = lax.ppermute(tensor, "narrow", sibling)

    tables = small_tables(*small, atoms)
    weight = weights((tensor,) * 3, (0, 1, 2), 1, atoms - 2, atoms, *tables)
    before, after, weight = after_of((before, after, weight))
    weight = weights((before, tensor, tensor), (0, 0, 1), 0, 1, atoms, *tables, weight)
    weight = weights(
        (tensor, tensor, after), (atoms - 2, atoms - 1, 0), atoms - 1, 1, atoms, *tables, weight
    )
    first = responses(tensor, weight)
    near, first, weight = after_of((near, first, weight))
    second = responses(near, weight)
    parts = {0: jnp.stack([first, second])}
    for step, held in direct.items():
        held, second, weight = after_of((held, second, weight))
        passed = lax.ppermute(held, "narrow", sibling)
        first = responses(held, weight)
        passed, first, weight = after_of((passed, first, weight))
        second = responses(passed, weight)
        parts[step] = jnp.stack([first, second])

    core = me % 2
    ordered = []
    for pair in range(narrow // 2):
        step = (me // 2 - pair) % (narrow // 2) * 2
        block = parts[0]
        for s in range(2, narrow, 2):
            block = jnp.where(step == s, parts[s], block)
        ordered.append(jnp.where(core == 0, block, block[::-1]))
    partial = jnp.concatenate(ordered, 0).reshape(wide, narrow * ri // wide, ri)
    return partial.astype(jnp.bfloat16)


def body(tensor, occupied, virtual, atom_size, tensor_pattern, occupied_pattern, virtual_pattern):
    partial = partial_response(
        tensor,
        occupied,
        virtual,
        atom_size,
        tensor_pattern,
        occupied_pattern,
        virtual_pattern,
    )
    shares = lax.all_to_all(partial, "wide", 0, 0, tiled=True)
    return jnp.sum(shares.astype(jnp.float32), 0)


def solution(mesh):
    placed = (P("wide", None, "narrow", None), P(), P(), P(), P(), P(), P())
    return jax.shard_map(
        body, mesh=mesh, in_specs=placed, out_specs=P("wide", "narrow"), check_vma=False
    )
```
